256 devices in a mesh: basis: 16 (over x_hi, z), ex: 16 (over y, x_lo, core).
Axes of the slice: x: 4 (x_hi: 2, x_lo: 2; x = x_hi * 2 + x_lo), y: 4, z: 8, core: 2. Of those that a mesh axis runs over, the one named last changes fastest.
Arguments:
- activations: bfloat16 [2048, 27648], P('ex', 'basis'), may hold values from -6 to 6
- out_grads: bfloat16 [2048, 5120], P('ex'), may hold values from -6 to 6
- act_basis: bfloat16 [27648, 18432], P('basis', 'ex'), may hold values from -0.0390625 to 0.0390625
- grad_basis: bfloat16 [5120, 5120], P(None, 'basis'), may hold values from -0.078125 to 0.078125
- ex_lengths: int32 [16, 5], replicated, may hold values from 1 to 36, 128 in all within a row
Outputs:
- eigenvalues: float32 [5120, 18432], P('basis', 'ex')
The draws below stay inside these ranges and needn't reach their ends.
Inputs may be any that keep to these rules, and one draw needn't show every extreme that they name: `ex_lengths`: each row sums to 128, and in every row some entry equals 36.
All inputs are finite; a program needn't handle non-finite values.
Results may differ from the reference program's by a relative error of at most 0.0014.
Values may be sent and summed in bfloat16 or wider, within the bound.
No kernel may reach another device: no remote copies, remote signals or barrier semaphores. Data moves between devices by JAX's collectives and lax.ppermute only.
A program may use at most 128 MiB of HBM per device.

```python
import math
import jax
import jax.numpy as jnp
import numpy as np
from jax import lax

D_IN = 27648
D_OUT = 5120
JC = 18432
TOK_EX = 128
EXB = 5
MOST = 36
TOKENS = 2048
N_EX = 16


def shard_levels(own_key, extent, shards, least, high):
    factor_of = 1.0
    for axis_at, parts in shards:
        steps = jax.random.uniform(jax.random.fold_in(jax.random.fold_in(own_key, 6), axis_at), (parts,), jnp.float32, least / len(shards), high / len(shards))
        factor_of = factor_of * jnp.repeat(jnp.exp(steps), extent[axis_at] // parts).reshape((-1,) + (1,) * (len(extent) - 1 - axis_at))
    return factor_of


def profile(amount, total, limit, slope):
    weights = [(1 << 20) // math.isqrt(rank ** slope) + 1 for rank in range(2, amount + 1)]
    spare, holding = total - limit - (amount - 1), [1] * (amount - 1)
    while spare > 0:
        candidates = [i for i in range(amount - 1) if holding[i] < limit]
        whole, remaining = sum([weights[i] for i in candidates]), spare
        for i in candidates:
            more = min(limit - holding[i], max(1, remaining * weights[i] // whole), spare)
            holding[i] = holding[i] + more
            spare = spare - more
    return np.array([limit] + holding)


def uneven(key, number_of, total, most, skew):
    if number_of == 2:
        one = jax.random.randint(key, (), max(1, total - most), min(most, total - 1) + 1)
        return jnp.stack([one, total - one])
    sizes = jnp.asarray(profile(number_of, total, most, skew), jnp.int32)
    pairs = (number_of - 1) // 2
    giver, taker = sizes[1:1 + 2 * pairs:2], sizes[2:2 + 2 * pairs:2]
    slack = jnp.minimum(giver - 1, most - taker)
    moved = jax.random.randint(jax.random.fold_in(key, 1), (pairs,), 0, 1 << 20) % (slack + 1)
    sizes = sizes.at[1:1 + 2 * pairs:2].set(giver - moved).at[2:2 + 2 * pairs:2].set(taker + moved)
    return sizes[jax.random.permutation(jax.random.fold_in(key, 2), number_of)]


def scatter_about(own_key, dims, deviation, limit, split=(), held_as=jnp.bfloat16):
    entries = deviation * jax.random.normal(own_key, dims, jnp.float32)
    if split:
        entries = entries * shard_levels(own_key, dims, split, -0.22, 0.18)
    return jnp.clip(entries, -limit, limit).astype(held_as)


def setup_inputs(seed: int = 0) -> dict:
    splits = jax.random.split(jax.random.key(seed), 6)
    activations = scatter_about(splits[0], (TOKENS, D_IN), 1.0, 6.0, ((0, 16), (1, 16)))
    out_grads = scatter_about(splits[1], (TOKENS, D_OUT), 1.0, 6.0, ((0, 16),))
    act_basis = scatter_about(splits[2], (D_IN, JC), D_IN ** -0.5, 0.0390625, ((0, 16), (1, 16)))
    grad_basis = scatter_about(splits[3], (D_OUT, D_OUT), D_OUT ** -0.5, 0.078125, ((1, 16),))
    ex_lengths = jax.vmap(lambda own: uneven(own, EXB, TOK_EX, MOST, 1))(jax.random.split(splits[4], N_EX)).reshape((N_EX, EXB)).astype(jnp.int32)
    return dict(activations=activations, out_grads=out_grads, act_basis=act_basis, grad_basis=grad_basis, ex_lengths=ex_lengths)


def reference(activations, out_grads, act_basis, grad_basis, ex_lengths):
    act_coeffs = jnp.dot(activations, act_basis, preferred_element_type=jnp.float32).astype(jnp.bfloat16)
    grad_coeffs = jnp.dot(out_grads, grad_basis, preferred_element_type=jnp.float32).astype(jnp.bfloat16)
    flat_lengths = ex_lengths.reshape(-1).astype(jnp.int32)
    end_points = jnp.cumsum(flat_lengths).astype(jnp.int32)
    starts = (end_points - flat_lengths).astype(jnp.int32)
    act_padded = jnp.concatenate([act_coeffs, jnp.zeros((MOST, JC), jnp.bfloat16)], axis=0)
    grad_padded = jnp.concatenate([grad_coeffs, jnp.zeros((MOST, D_OUT), jnp.bfloat16)], axis=0)
    offsets = jnp.arange(MOST, dtype=jnp.int32)

    def scan_step(accumulated, example):
        begin_at, length_of = example
        slot_keep = (offsets < length_of).astype(jnp.bfloat16)[:, None]
        rows_act = lax.dynamic_slice_in_dim(act_padded, begin_at, MOST, 0) * slot_keep
        rows_grad = lax.dynamic_slice_in_dim(grad_padded, begin_at, MOST, 0) * slot_keep
        coeffs = jnp.dot(rows_grad.T, rows_act, preferred_element_type=jnp.float32)
        return accumulated + coeffs * coeffs, None

    accumulated, _ = lax.scan(scan_step, jnp.zeros((D_OUT, JC), jnp.float32), (starts, flat_lengths))
    return accumulated / jnp.float32(TOKENS)
```

```python
import jax
import jax.numpy as jnp
from jax import lax
from jax.experimental import pallas as pl
from jax.experimental.pallas import tpu as pltpu
from jax.sharding import PartitionSpec as P

Z, X_HI = 8, 2
Y, X_LO, CORE = 4, 2, 2
BLOCK = 128
EXB = 5
WIDE = 256


def shift_z(value, by):
    pairs = [(x * Z + z, x * Z + (z + by) % Z) for x in range(X_HI) for z in range(Z)]
    return lax.ppermute(value, "basis", pairs)


def swap_x(value):
    pairs = [(x * Z + z, (1 - x) * Z + z) for x in range(X_HI) for z in range(Z)]
    return lax.ppermute(value, "basis", pairs)


def ex_index(y, x, c):
    return (y * X_LO + x) * CORE + c


def shift_ex(value, dy, dx, dc):
    pairs = [
        (ex_index(y, x, c), ex_index((y + dy) % Y, (x + dx) % X_LO, (c + dc) % CORE))
        for y in range(Y)
        for x in range(X_LO)
        for c in range(CORE)
    ]
    return lax.ppermute(value, "ex", pairs)


def both_cores(parts):
    mine = jnp.concatenate(parts, axis=0) if len(parts) > 1 else parts[0]
    return [mine, shift_ex(mine, 0, 0, 1)]


def gather_groups(own):
    rows = own.shape[0]
    up, down, side = (0, 1), (0, -1), (1, 0)
    first_y = shift_ex(own, 1, 0, 0)
    second_y = shift_ex(own, -1, 0, 0)
    beside = shift_ex(own, 0, 1, 0)
    far = shift_ex(first_y, 1, 0, 0)
    beside_up = shift_ex(beside, -1, 0, 0)
    beside_down = shift_ex(first_y, 0, 1, 0)
    a, b = 48, 96
    last = [
        shift_ex(beside_down[:a], 1, 0, 0),
        shift_ex(beside_up[a:b], -1, 0, 0),
        shift_ex(far[b:], 0, 1, 0),
    ]
    groups = [[own], [first_y, second_y, beside], [far, beside_up, beside_down], [jnp.concatenate(last, 0)]]
    places = [[(0, 0)], [(-1, 0), (1, 0), (0, 1)], [(2, 0), (1, 1), (-1, 1)], [(2, 1)]]
    arrays, order = [], []
    for parts, place in zip(groups, places):
        arrays.append(both_cores(parts))
        order.append([(dy, dx, dc) for dc in range(CORE) for dy, dx in place])
    return arrays, order


def sum_over_basis(partial_of, chunk):
    bf = jnp.bfloat16
    half = chunk // 2
    farthest = partial_of(4).astype(bf)
    going_down = shift_z(farthest[:half], -1)
    going_up = shift_z(farthest[half:], 1)
    for k in (3, 2, 1):
        low, high = partial_of(-k), partial_of(k)
        if k == 3:
            low = jnp.concatenate([low[:half] + going_down, low[half:]], 0)
            high = jnp.concatenate([high[:half], high[half:] + going_up], 0)
        else:
            low, high = low + going_down, high + going_up
        going_down = shift_z(low.astype(bf), -1)
        going_up = shift_z(high.astype(bf), 1)
    total = partial_of(0) + going_down + going_up
    return (total + swap_x(total.astype(bf))).astype(bf)


def gather_over_z(value):
    groups = [[x * Z + z for z in range(Z)] for x in range(X_HI)]
    return lax.all_gather(value, "basis", axis=0, tiled=True, axis_index_groups=groups)


def outer_kernel(scale, at_ref, bounds_ref, grad_ref, act_ref, out_ref):
    blocks, high, block = grad_ref.shape
    wide = act_ref.shape[1]
    token = lax.broadcasted_iota(jnp.int32, (high, block), 1)
    out_ref[...] = jnp.zeros_like(out_ref)

    def step(b, carry):
        at = at_ref[b]
        grads = grad_ref[at]
        zeros = jnp.zeros_like(grads)
        rows = pl.ds(pl.multiple_of(b * block, block), block)
        lhs = jnp.concatenate(
            [
                jnp.where((token >= bounds_ref[at, e]) & (token < bounds_ref[at, e + 1]), grads, zeros)
                for e in range(EXB)
            ],
            axis=0,
        )
        for n in range(0, wide, WIDE):
            columns = slice(n, min(n + WIDE, wide))
            coeffs = jnp.dot(lhs, act_ref[rows, columns], preferred_element_type=jnp.float32)
            squares = coeffs * coeffs
            total = squares[:high]
            for e in range(1, EXB):
                total = total + squares[e * high : (e + 1) * high]
            out_ref[:, columns] += total
        return carry

    lax.fori_loop(0, blocks, step, 0, unroll=2)
    out_ref[...] = out_ref[...] * scale


def squared_sums(at, bounds, grads, acts, token_count):
    vmem = pl.BlockSpec(memory_space=pltpu.VMEM)
    smem = pl.BlockSpec(memory_space=pltpu.SMEM)
    blocks, high, block = grads.shape
    return pl.pallas_call(
        lambda *refs: outer_kernel(1.0 / token_count, *refs),
        out_shape=jax.ShapeDtypeStruct((high, acts.shape[1]), jnp.float32),
        in_specs=[smem, smem, vmem, vmem],
        out_specs=vmem,
        compiler_params=pltpu.CompilerParams(vmem_limit_bytes=40 * 1024 * 1024),
        cost_estimate=pl.CostEstimate(
            flops=2 * EXB * acts.size * high, bytes_accessed=2 * acts.size, transcendentals=0
        ),
    )(at, bounds, grads, acts)


def on_device(activations, out_grads, act_basis, grad_basis, ex_lengths):
    token_count = out_grads.shape[0] * lax.axis_size("ex")
    z = lax.axis_index("basis") % Z
    ex = lax.axis_index("ex")
    y, x, c = ex // (X_LO * CORE), (ex // CORE) % X_LO, ex % CORE

    grad_local = lax.dot_general(
        grad_basis, out_grads, (((0,), (1,)), ((), ())), preferred_element_type=jnp.float32
    ).astype(jnp.bfloat16)
    grads = lax.all_gather(grad_local, "ex", axis=0)

    arrays, order = gather_groups(activations)
    arrays[-1], grads = lax.optimization_barrier((arrays[-1], grads))
    streams = STREAMS
    acts, places = [], []
    for stream in streams:
        tokens = jnp.concatenate([a for g in stream for a in arrays[g]], axis=0)
        for g in stream:
            places += order[g]
        chunk = tokens.shape[0] // Z

        def partial_of(k, tokens=tokens, chunk=chunk):
            rows = lax.dynamic_slice_in_dim(tokens, ((z + k) % Z) * chunk, chunk, 0)
            return jnp.dot(rows, act_basis, preferred_element_type=jnp.float32)

        acts.append(gather_over_z(sum_over_basis(partial_of, chunk)))

    at = jnp.stack(
        [((y + dy) % Y * X_LO + (x + dx) % X_LO) * CORE + (c + dc) % CORE for dy, dx, dc in places]
    ).astype(jnp.int32)
    ends = jnp.cumsum(ex_lengths, axis=1)
    bounds = jnp.concatenate([jnp.zeros_like(ends[:, :1]), ends], axis=1).astype(jnp.int32)
    act_coeffs = jnp.concatenate(acts, axis=0) if len(acts) > 1 else acts[0]
    return squared_sums(at, bounds, grads, act_coeffs, token_count)


STREAMS = ((0, 1, 2, 3),)


def solution(mesh):
    in_specs = (P("ex", "basis"), P("ex", None), P("basis", "ex"), P(None, "basis"), P())
    out_specs = P("basis", "ex")
    return jax.shard_map(
        on_device, mesh=mesh, in_specs=in_specs, out_specs=out_specs, check_vma=False
    )
```

```python
import jax
import jax.numpy as jnp
from jax import lax
from jax.experimental import pallas as pl
from jax.experimental.pallas import tpu as pltpu
from jax.sharding import PartitionSpec as P

Z, X_HI = 8, 2
Y, X_LO, CORE = 4, 2, 2
BLOCK = 128
HALF = BLOCK // 2
EXB = 5
WIDE = 256
bf16, f32 = jnp.bfloat16, jnp.float32
LITTLE = pl.CostEstimate(flops=1, bytes_accessed=1, transcendentals=0)
VMEM = pl.BlockSpec(memory_space=pltpu.VMEM)
SMEM = pl.BlockSpec(memory_space=pltpu.SMEM)
ANY = pl.BlockSpec(memory_space=pl.ANY)


class Order:
    def __init__(self, token):
        self.token = token

    def __call__(self, *values):
        *values, self.token = lax.optimization_barrier((*values, self.token))
        return values


def shift_z(value, by):
    pairs = [(x * Z + z, x * Z + (z + by) % Z) for x in range(X_HI) for z in range(Z)]
    return lax.ppermute(value, "basis", pairs)


def swap_x(value):
    pairs = [(x * Z + z, (1 - x) * Z + z) for x in range(X_HI) for z in range(Z)]
    return lax.ppermute(value, "basis", pairs)


def ex_index(y, x, c):
    return (y * X_LO + x) * CORE + c


def shift_ex(value, dy, dx, dc):
    pairs = [
        (ex_index(y, x, c), ex_index((y + dy) % Y, (x + dx) % X_LO, (c + dc) % CORE))
        for y in range(Y)
        for x in range(X_LO)
        for c in range(CORE)
    ]
    return lax.ppermute(value, "ex", pairs)


def other_core(value):
    return shift_ex(value, 0, 0, 1)


def widen_kernel(in_ref, out_ref):
    depth, rows = in_ref.shape
    for at in range(0, out_ref.shape[1], BLOCK):
        have = max(0, min(BLOCK, depth - at))
        parts = [in_ref[at : at + have, :]] if have else []
        if have < BLOCK:
            parts.append(jnp.zeros((BLOCK - have, rows), in_ref.dtype))
        part = jnp.concatenate(parts, 0) if len(parts) > 1 else parts[0]
        out_ref[:, at : at + BLOCK] = part.T


def widen(activations):
    rows, depth = activations.shape
    return pl.pallas_call(
        widen_kernel,
        out_shape=jax.ShapeDtypeStruct((rows, depth + -depth % WIDE), activations.dtype),
        in_specs=[VMEM],
        out_specs=VMEM,
        cost_estimate=LITTLE,
    )(activations.T)


def project_kernel(where_ref, *refs):
    count = len(refs) - 5
    pieces, basis_ref, farthest_ref, shares_ref, held, sems = refs[:count], *refs[count:]
    z = where_ref[3]
    row, blocks = 0, {}
    for i, piece in enumerate(pieces):
        load = pltpu.make_async_copy(piece, held.at[row : row + piece.shape[0]], sems.at[i])
        load.start()
        blocks.setdefault(row // BLOCK, []).append(load)
        row += piece.shape[0]
    for block, loads in blocks.items():
        for load in loads:
            load.wait()
        tokens = held[block * BLOCK : (block + 1) * BLOCK]
        place = lax.rem(block - z + 3 + Z, Z)
        shares_ref[pl.ds(pl.multiple_of(place * BLOCK, BLOCK), BLOCK), :] = jnp.dot(
            tokens, basis_ref[...], preferred_element_type=f32
        )
    farthest_ref[...] = shares_ref[(Z - 1) * BLOCK :, :].astype(bf16)


def project(where, pieces, basis):
    rows = sum(piece.shape[0] for piece in pieces)
    depth, wide = basis.shape
    return pl.pallas_call(
        project_kernel,
        out_shape=[jax.ShapeDtypeStruct((BLOCK, wide), bf16), jax.ShapeDtypeStruct((rows, wide), f32)],
        in_specs=[SMEM] + [ANY] * len(pieces) + [VMEM],
        out_specs=[VMEM, VMEM],
        scratch_shapes=[pltpu.VMEM((rows, depth), bf16), pltpu.SemaphoreType.DMA((len(pieces),))],
        compiler_params=pltpu.CompilerParams(vmem_limit_bytes=24 * 1024 * 1024),
        cost_estimate=LITTLE,
    )(where, *pieces, basis)


class Stream:
    def __init__(self, order, farthest, shares):
        self.order = order
        self.farthest = farthest
        self.shares = shares
        self.left = 4
        self.blocks = {}

    def share(self, k):
        place = (k + 3) % Z
        return self.shares[place * BLOCK : (place + 1) * BLOCK]

    def reduce(self):
        k = self.left
        if k == 4:
            low, high = self.farthest[:HALF], self.farthest[HALF:]
        else:
            down, up = self.order(self.down, self.up)
            low, high = self.share(-k), self.share(k)
            if k == 3:
                low = jnp.concatenate([low[:HALF] + down, low[HALF:]], 0)
                high = jnp.concatenate([high[:HALF], high[HALF:] + up], 0)
            else:
                low, high = low + down, high + up
            low, high = low.astype(bf16), high.astype(bf16)
        low, high = self.order(low, high)
        self.down, self.up = shift_z(low, -1), shift_z(high, 1)
        self.left -= 1

    def cross(self):
        down, up = self.order(self.down, self.up)
        self.total = self.share(0) + down + up
        (sent,) = self.order(self.total.astype(bf16))
        self.crossed = swap_x(sent)

    def finish(self):
        (crossed,) = self.order(self.crossed)
        (own,) = self.order((self.total + crossed).astype(bf16))
        self.blocks[0] = own
        self.down, self.up = shift_z(own, -1), shift_z(own, 1)
        self.step = 1

    def spread(self):
        k = self.step
        down, up = self.order(self.down, self.up)
        self.blocks[k], self.blocks[-k] = down, up
        if k == 3:
            down, up = down[:HALF], up[HALF:]
        self.down, self.up = shift_z(down, -1), shift_z(up, 1)
        self.step += 1

    def arrive(self):
        self.blocks[4] = tuple(self.order(self.down, self.up))


def outer_kernel(scale, which, earlier, parts_of, where_ref, lengths_ref, *refs):
    places_ref, grads_hbm = refs[0], refs[1]
    number = sum(parts_of)
    acts_hbm = refs[2 : 2 + number]
    out_ref, grads_ref, acts_ref, grad_sems, act_sems, out_sem = refs[-6:]
    high, block = grads_ref.shape[1:]
    y, x, c, z = (where_ref[i] for i in range(4))
    if earlier:
        resume = pltpu.make_async_copy(refs[2 + number], out_ref, out_sem.at[0])
    ats, copies, first = [], [], 0
    for i, (s, k) in enumerate(which):
        place = lax.rem(z + k + Z, Z) + s * Z
        at = lax.rem(y + places_ref[place, 0] + Y, Y) * X_LO + lax.rem(x + places_ref[place, 1], X_LO)
        at = at * CORE + lax.rem(c + places_ref[place, 2], CORE)
        own = [pltpu.make_async_copy(grads_hbm.at[at], grads_ref.at[i], grad_sems.at[i])]
        row = i * block
        for act in acts_hbm[first : first + parts_of[i]]:
            own.append(pltpu.make_async_copy(act, acts_ref.at[row : row + act.shape[0]], act_sems.at[first]))
            row += act.shape[0]
            first += 1
        for copy in own:
            copy.start()
        if earlier and i == 0:
            resume.start()
        ats.append(at)
        copies.append(own)
    token = lax.broadcasted_iota(jnp.int32, (high, block), 1)
    for i, at in enumerate(ats):
        for copy in copies[i]:
            copy.wait()
        grads = grads_ref[i]
        zeros = jnp.zeros_like(grads)
        masked, begin = [], jnp.int32(0)
        for e in range(EXB):
            end = begin + lengths_ref[at, e]
            masked.append(jnp.where((token >= begin) & (token < end), grads, zeros))
            begin = end
        lhs = jnp.concatenate(masked, axis=0)
        if earlier and i == 0:
            resume.wait()
        for n in range(0, out_ref.shape[1], WIDE):
            columns = slice(n, min(n + WIDE, out_ref.shape[1]))
            rhs = acts_ref[i * block : (i + 1) * block, columns]
            coeffs = jnp.dot(lhs, rhs, preferred_element_type=f32)
            squares = coeffs * coeffs
            total = squares[:high]
            for e in range(1, EXB):
                total = total + squares[e * high : (e + 1) * high]
            if i or earlier:
                total = total + out_ref[:, columns]
            if scale is not None and i == len(ats) - 1:
                total = total * scale
            out_ref[:, columns] = total


def squared_sums(which, where, places, streams, lengths, grads, earlier, scale=None):
    _, high, block = grads.shape
    parts = [p if isinstance(p, tuple) else (p,) for p in (streams[s].blocks[k] for s, k in which)]
    parts_of = tuple(len(p) for p in parts)
    acts = [a for p in parts for a in p]
    wide = acts[0].shape[1]
    earlier = [] if earlier is None else [earlier]
    places = jnp.array(places, jnp.int32)
    return pl.pallas_call(
        lambda *refs: outer_kernel(scale, which, bool(earlier), parts_of, *refs),
        out_shape=jax.ShapeDtypeStruct((high, wide), f32),
        in_specs=[SMEM] * 3 + [ANY] * (1 + len(acts) + len(earlier)),
        out_specs=VMEM,
        scratch_shapes=[
            pltpu.VMEM((len(which), high, block), bf16),
            pltpu.VMEM((len(which) * block, wide), bf16),
            pltpu.SemaphoreType.DMA((len(which),)),
            pltpu.SemaphoreType.DMA((len(acts),)),
            pltpu.SemaphoreType.DMA((1,)),
        ],
        compiler_params=pltpu.CompilerParams(vmem_limit_bytes=16 * 1024 * 1024),
        cost_estimate=LITTLE,
    )(where, lengths, places, grads, *acts, *earlier)


def on_device(activations, out_grads, act_basis, grad_basis, ex_lengths):
    token_count = out_grads.shape[0] * lax.axis_size("ex")
    z = lax.axis_index("basis") % Z
    ex = lax.axis_index("ex")
    where = jnp.stack([ex // (X_LO * CORE), (ex // CORE) % X_LO, ex % CORE, z]).astype(jnp.int32)
    lengths = ex_lengths.astype(jnp.int32)

    order = Order(where)

    own = widen(activations)
    from_down = shift_ex(own, 1, 0, 0)
    from_up = shift_ex(own, -1, 0, 0)
    beside = shift_ex(own, 0, 1, 0)
    own_other = other_core(own)
    grad_local = lax.dot_general(
        grad_basis, out_grads, (((0,), (1,)), ((), ())), preferred_element_type=f32
    ).astype(bf16)
    basis = jnp.pad(act_basis, ((0, own.shape[1] - act_basis.shape[0]), (0, 0)))
    grad_local, basis = order(grad_local, basis)
    from_down, from_up, beside = order(from_down, from_up, beside)
    far = shift_ex(from_down, 1, 0, 0)
    beside_up = shift_ex(beside, -1, 0, 0)
    beside_down = shift_ex(from_down, 0, 1, 0)
    second = [from_down, from_up, beside]
    second_other = [other_core(p) for p in second]
    a = Stream(order, *order(*project(where, [own, own_other, *second, *second_other], basis)))
    far, beside_up, beside_down = order(far, beside_up, beside_down)
    last = order(beside_down[:HALF], beside_up[HALF:])
    last = [shift_ex(last[0], 1, 0, 0), shift_ex(last[1], -1, 0, 0)]
    third = [far, beside_up, beside_down]
    third_other = [other_core(p) for p in third]
    a.reduce()
    last = order(*last)
    last_other = [other_core(p) for p in last]
    a.reduce()
    (grad_local,) = order(grad_local)
    grads = lax.all_gather(grad_local, "ex", axis=0)
    b = Stream(order, *order(*project(where, [*third, *third_other, *last, *last_other], basis)))

    streams = a, b
    ring = [(0, 0)], [(-1, 0), (1, 0), (0, 1)], [(2, 0), (1, 1), (-1, 1)], [(2, 1)]
    places = [(dy, dx, dc) for group in ring for dc in range(CORE) for dy, dx in group]
    total = None

    def add(which, scale=None):
        (total_then,) = order(
            squared_sums(which, order.token, places, streams, lengths, grads, total, scale)
        )
        return total_then

    b.reduce()
    a.reduce()
    b.reduce()
    a.reduce()
    b.reduce()
    a.cross()
    b.reduce()
    a.finish()
    b.cross()
    a.spread()
    b.finish()
    (grads,) = order(grads)
    total = add(((0, 0), (0, 1), (0, -1), (1, 0)))
    for k in (2, 3):
        a.spread()
        b.spread()
        total = add(((0, k), (0, -k), (1, k - 1), (1, 1 - k)))
    a.arrive()
    b.spread()
    total = add(((0, 4), (1, 3), (1, -3)))
    b.arrive()
    return add(((1, 4),), 1.0 / token_count)


def solution(mesh):
    in_specs = (P("ex", "basis"), P("ex", None), P("basis", "ex"), P(None, "basis"), P())
    out_specs = P("basis", "ex")
    return jax.shard_map(
        on_device, mesh=mesh, in_specs=in_specs, out_specs=out_specs, check_vma=False
    )
```

```python
import jax
import jax.numpy as jnp
from jax import lax
from jax.experimental import pallas as pl
from jax.experimental.pallas import tpu as pltpu
from jax.sharding import PartitionSpec as P

Z, X_HI = 8, 2
Y, X_LO, CORE = 4, 2, 2
BLOCK = 128
HALF = BLOCK // 2
EXB = 5
WIDE = 256
bf16, f32 = jnp.bfloat16, jnp.float32
LITTLE = pl.CostEstimate(flops=1, bytes_accessed=1, transcendentals=0)
VMEM = pl.BlockSpec(memory_space=pltpu.VMEM)
SMEM = pl.BlockSpec(memory_space=pltpu.SMEM)
ANY = pl.BlockSpec(memory_space=pl.ANY)


class Order:
    def __init__(self, token):
        self.token = token

    def __call__(self, *values):
        *values, self.token = lax.optimization_barrier((*values, self.token))
        return values


def shift_z(value, by):
    pairs = [(x * Z + z, x * Z + (z + by) % Z) for x in range(X_HI) for z in range(Z)]
    return lax.ppermute(value, "basis", pairs)


def swap_x(value):
    pairs = [(x * Z + z, (1 - x) * Z + z) for x in range(X_HI) for z in range(Z)]
    return lax.ppermute(value, "basis", pairs)


def ex_index(y, x, c):
    return (y * X_LO + x) * CORE + c


def shift_ex(value, dy, dx, dc):
    pairs = [
        (ex_index(y, x, c), ex_index((y + dy) % Y, (x + dx) % X_LO, (c + dc) % CORE))
        for y in range(Y)
        for x in range(X_LO)
        for c in range(CORE)
    ]
    return lax.ppermute(value, "ex", pairs)


def other_core(value):
    return shift_ex(value, 0, 0, 1)


def widen_kernel(in_ref, out_ref):
    depth, rows = in_ref.shape
    for at in range(0, out_ref.shape[1], BLOCK):
        have = max(0, min(BLOCK, depth - at))
        parts = [in_ref[at : at + have, :]] if have else []
        if have < BLOCK:
            parts.append(jnp.zeros((BLOCK - have, rows), in_ref.dtype))
        part = jnp.concatenate(parts, 0) if len(parts) > 1 else parts[0]
        out_ref[:, at : at + BLOCK] = part.T


def widen(activations):
    rows, depth = activations.shape
    return pl.pallas_call(
        widen_kernel,
        out_shape=jax.ShapeDtypeStruct((rows, depth + -depth % WIDE), activations.dtype),
        in_specs=[VMEM],
        out_specs=VMEM,
        cost_estimate=LITTLE,
    )(activations.T)


def project_kernel(where_ref, *refs):
    count = len(refs) - 5
    pieces, basis_ref, farthest_ref, shares_ref, held, sems = refs[:count], *refs[count:]
    z = where_ref[3]
    row, blocks = 0, {}
    for i, piece in enumerate(pieces):
        load = pltpu.make_async_copy(piece, held.at[row : row + piece.shape[0]], sems.at[i])
        load.start()
        blocks.setdefault(row // BLOCK, []).append(load)
        row += piece.shape[0]
    for block, loads in blocks.items():
        for load in loads:
            load.wait()
        tokens = held[block * BLOCK : (block + 1) * BLOCK]
        place = lax.rem(block - z + 3 + Z, Z)
        shares_ref[pl.ds(pl.multiple_of(place * BLOCK, BLOCK), BLOCK), :] = jnp.dot(
            tokens, basis_ref[...], preferred_element_type=f32
        )
    farthest_ref[...] = shares_ref[(Z - 1) * BLOCK :, :].astype(bf16)


def project(where, pieces, basis):
    rows = sum(piece.shape[0] for piece in pieces)
    depth, wide = basis.shape
    return pl.pallas_call(
        project_kernel,
        out_shape=[jax.ShapeDtypeStruct((BLOCK, wide), bf16), jax.ShapeDtypeStruct((rows, wide), f32)],
        in_specs=[SMEM] + [ANY] * len(pieces) + [VMEM],
        out_specs=[VMEM, VMEM],
        scratch_shapes=[pltpu.VMEM((rows, depth), bf16), pltpu.SemaphoreType.DMA((len(pieces),))],
        compiler_params=pltpu.CompilerParams(vmem_limit_bytes=24 * 1024 * 1024),
        cost_estimate=LITTLE,
    )(where, *pieces, basis)


class Stream:
    def __init__(self, order, farthest, shares):
        self.order = order
        self.farthest = farthest
        self.shares = shares
        self.left = 4
        self.blocks = {}

    def share(self, k):
        place = (k + 3) % Z
        return self.shares[place * BLOCK : (place + 1) * BLOCK]

    def reduce(self):
        k = self.left
        if k == 4:
            low, high = self.farthest[:HALF], self.farthest[HALF:]
        else:
            down, up = self.order(self.down, self.up)
            low, high = self.share(-k), self.share(k)
            if k == 3:
                low = jnp.concatenate([low[:HALF] + down, low[HALF:]], 0)
                high = jnp.concatenate([high[:HALF], high[HALF:] + up], 0)
            else:
                low, high = low + down, high + up
            low, high = low.astype(bf16), high.astype(bf16)
        low, high = self.order(low, high)
        self.down, self.up = shift_z(low, -1), shift_z(high, 1)
        self.left -= 1

    def cross(self):
        down, up = self.order(self.down, self.up)
        self.total = self.share(0) + down + up
        (sent,) = self.order(self.total.astype(bf16))
        self.crossed = swap_x(sent)

    def finish(self):
        (crossed,) = self.order(self.crossed)
        (own,) = self.order((self.total + crossed).astype(bf16))
        self.blocks[0] = own
        self.down, self.up = shift_z(own, -1), shift_z(own, 1)
        self.step = 1

    def spread(self):
        k = self.step
        down, up = self.order(self.down, self.up)
        self.blocks[k], self.blocks[-k] = down, up
        if k == 3:
            down, up = down[:HALF], up[HALF:]
        self.down, self.up = shift_z(down, -1), shift_z(up, 1)
        self.step += 1

    def arrive(self):
        self.blocks[4] = tuple(self.order(self.down, self.up))


def outer_kernel(scale, which, earlier, parts_of, where_ref, lengths_ref, *refs):
    places_ref, grads_hbm = refs[0], refs[1]
    number = sum(parts_of)
    acts_hbm = refs[2 : 2 + number]
    out_ref, grads_ref, acts_ref, grad_sems, act_sems, out_sem = refs[-6:]
    high, block = grads_ref.shape[1:]
    y, x, c, z = (where_ref[i] for i in range(4))
    if earlier:
        resume = pltpu.make_async_copy(refs[2 + number], out_ref, out_sem.at[0])
    ats, copies, first = [], [], 0
    for i, (s, k) in enumerate(which):
        place = lax.rem(z + k + Z, Z) + s * Z
        at = lax.rem(y + places_ref[place, 0] + Y, Y) * X_LO + lax.rem(x + places_ref[place, 1], X_LO)
        at = at * CORE + lax.rem(c + places_ref[place, 2], CORE)
        own = [pltpu.make_async_copy(grads_hbm.at[places_ref[place, 3]], grads_ref.at[i], grad_sems.at[i])]
        row = i * block
        for act in acts_hbm[first : first + parts_of[i]]:
            own.append(pltpu.make_async_copy(act, acts_ref.at[row : row + act.shape[0]], act_sems.at[first]))
            row += act.shape[0]
            first += 1
        for copy in own:
            copy.start()
        if earlier and i == 0:
            resume.start()
        ats.append(at)
        copies.append(own)
    token = lax.broadcasted_iota(jnp.int32, (high, block), 1)
    for i, at in enumerate(ats):
        for copy in copies[i]:
            copy.wait()
        grads = grads_ref[i]
        zeros = jnp.zeros_like(grads)
        masked, begin = [], jnp.int32(0)
        for e in range(EXB):
            end = begin + lengths_ref[at, e]
            masked.append(jnp.where((token >= begin) & (token < end), grads, zeros))
            begin = end
        lhs = jnp.concatenate(masked, axis=0)
        if earlier and i == 0:
            resume.wait()
        for n in range(0, out_ref.shape[1], WIDE):
            columns = slice(n, min(n + WIDE, out_ref.shape[1]))
            rhs = acts_ref[i * block : (i + 1) * block, columns]
            coeffs = jnp.dot(lhs, rhs, preferred_element_type=f32)
            squares = coeffs * coeffs
            total = squares[:high]
            for e in range(1, EXB):
                total = total + squares[e * high : (e + 1) * high]
            if i or earlier:
                total = total + out_ref[:, columns]
            if scale is not None and i == len(ats) - 1:
                total = total * scale
            out_ref[:, columns] = total


def squared_sums(which, where, places, streams, lengths, grads, earlier, scale=None):
    _, high, block = grads.shape
    parts = [p if isinstance(p, tuple) else (p,) for p in (streams[s].blocks[k] for s, k in which)]
    parts_of = tuple(len(p) for p in parts)
    acts = [a for p in parts for a in p]
    wide = acts[0].shape[1]
    earlier = [] if earlier is None else [earlier]
    places = jnp.array(places, jnp.int32)
    return pl.pallas_call(
        lambda *refs: outer_kernel(scale, which, bool(earlier), parts_of, *refs),
        out_shape=jax.ShapeDtypeStruct((high, wide), f32),
        in_specs=[SMEM] * 3 + [ANY] * (1 + len(acts) + len(earlier)),
        out_specs=VMEM,
        scratch_shapes=[
            pltpu.VMEM((len(which), high, block), bf16),
            pltpu.VMEM((len(which) * block, wide), bf16),
            pltpu.SemaphoreType.DMA((len(which),)),
            pltpu.SemaphoreType.DMA((len(acts),)),
            pltpu.SemaphoreType.DMA((1,)),
        ],
        compiler_params=pltpu.CompilerParams(vmem_limit_bytes=16 * 1024 * 1024),
        cost_estimate=LITTLE,
    )(where, lengths, places, grads, *acts, *earlier)


def on_device(activations, out_grads, act_basis, grad_basis, ex_lengths):
    token_count = out_grads.shape[0] * lax.axis_size("ex")
    z = lax.axis_index("basis") % Z
    ex = lax.axis_index("ex")
    where = jnp.stack([ex // (X_LO * CORE), (ex // CORE) % X_LO, ex % CORE, z]).astype(jnp.int32)
    lengths = ex_lengths.astype(jnp.int32)

    order = Order(where)

    own = widen(activations)
    from_down = shift_ex(own, 1, 0, 0)
    from_up = shift_ex(own, -1, 0, 0)
    beside = shift_ex(own, 0, 1, 0)
    own_other = other_core(own)
    grad_local = lax.dot_general(
        grad_basis, out_grads, (((0,), (1,)), ((), ())), preferred_element_type=f32
    ).astype(bf16)
    basis = jnp.pad(act_basis, ((0, own.shape[1] - act_basis.shape[0]), (0, 0)))
    grad_local, basis = order(grad_local, basis)
    from_down, from_up, beside = order(from_down, from_up, beside)
    far = shift_ex(from_down, 1, 0, 0)
    beside_up = shift_ex(beside, -1, 0, 0)
    beside_down = shift_ex(from_down, 0, 1, 0)
    second = [from_down, from_up, beside]
    second_other = [other_core(p) for p in second]
    a = Stream(order, *order(*project(where, [own, own_other, *second, *second_other], basis)))
    grad_beside = shift_ex(grad_local, 0, 1, 0)
    far, beside_up, beside_down = order(far, beside_up, beside_down)
    last = order(beside_down[:HALF], beside_up[HALF:])
    last = [shift_ex(last[0], 1, 0, 0), shift_ex(last[1], -1, 0, 0)]
    third = [far, beside_up, beside_down]
    third_other = [other_core(p) for p in third]
    a.reduce()
    (grad_beside,) = order(grad_beside)
    grads = jnp.stack([grad_local, grad_beside])
    grads_other = other_core(grads)
    last = order(*last)
    last_other = [other_core(p) for p in last]
    a.reduce()
    b = Stream(order, *order(*project(where, [*third, *third_other, *last, *last_other], basis)))

    streams = a, b
    ring = [(0, 0)], [(-1, 0), (1, 0), (0, 1)], [(2, 0), (1, 1), (-1, 1)], [(2, 1)]
    held = {0: 0, -1: 1, 1: 2, 2: 3}
    places = [
        (dy, dx, dc, (held[dy] * CORE + dc) * X_LO + dx)
        for group in ring
        for dc in range(CORE)
        for dy, dx in group
    ]
    total = None

    def add(which, scale=None):
        (total_then,) = order(
            squared_sums(which, order.token, places, streams, lengths, grads, total, scale)
        )
        return total_then

    b.reduce()
    a.reduce()
    (grads_other,) = order(grads_other)
    grads = jnp.concatenate([grads, grads_other], 0)
    grads_down, grads_up = shift_ex(grads, 1, 0, 0), shift_ex(grads, -1, 0, 0)
    b.reduce()
    a.reduce()
    grads_down, grads_up = order(grads_down, grads_up)
    grads_far = shift_ex(grads_down, 1, 0, 0)
    b.reduce()
    a.cross()
    b.reduce()
    a.finish()
    (grads_far,) = order(grads_far)
    grads = jnp.concatenate([grads, grads_down, grads_up, grads_far], 0)
    b.cross()
    a.spread()
    b.finish()
    total = add(((0, 0), (0, 1), (0, -1), (1, 0)))
    for k in (2, 3):
        a.spread()
        b.spread()
        total = add(((0, k), (0, -k), (1, k - 1), (1, 1 - k)))
    a.arrive()
    b.spread()
    total = add(((0, 4), (1, 3), (1, -3)))
    b.arrive()
    return add(((1, 4),), 1.0 / token_count)


def solution(mesh):
    in_specs = (P("ex", "basis"), P("ex", None), P("basis", "ex"), P(None, "basis"), P())
    out_specs = P("basis", "ex")
    return jax.shard_map(
        on_device, mesh=mesh, in_specs=in_specs, out_specs=out_specs, check_vma=False
    )
```

```python
import jax
import jax.numpy as jnp
from jax import lax
from jax.experimental import pallas as pl
from jax.experimental.pallas import tpu as pltpu
from jax.sharding import PartitionSpec as P

Z, X_HI = 8, 2
Y, X_LO, CORE = 4, 2, 2
BLOCK = 128
HALF = BLOCK // 2
EXB = 5
WIDE = 256
bf16, f32 = jnp.bfloat16, jnp.float32
LITTLE = pl.CostEstimate(flops=1, bytes_accessed=1, transcendentals=0)
VMEM = pl.BlockSpec(memory_space=pltpu.VMEM)
SMEM = pl.BlockSpec(memory_space=pltpu.SMEM)
ANY = pl.BlockSpec(memory_space=pl.ANY)


class Order:
    def __init__(self, token):
        self.token = token

    def __call__(self, *values):
        *values, self.token = lax.optimization_barrier((*values, self.token))
        return values


def shift_z(value, by):
    pairs = [(x * Z + z, x * Z + (z + by) % Z) for x in range(X_HI) for z in range(Z)]
    return lax.ppermute(value, "basis", pairs)


def swap_x(value):
    pairs = [(x * Z + z, (1 - x) * Z + z) for x in range(X_HI) for z in range(Z)]
    return lax.ppermute(value, "basis", pairs)


def ex_index(y, x, c):
    return (y * X_LO + x) * CORE + c


def shift_ex(value, dy, dx, dc):
    pairs = [
        (ex_index(y, x, c), ex_index((y + dy) % Y, (x + dx) % X_LO, (c + dc) % CORE))
        for y in range(Y)
        for x in range(X_LO)
        for c in range(CORE)
    ]
    return lax.ppermute(value, "ex", pairs)


def other_core(value):
    return shift_ex(value, 0, 0, 1)


def widen_kernel(in_ref, out_ref):
    depth, rows = in_ref.shape
    for at in range(0, out_ref.shape[1], BLOCK):
        have = max(0, min(BLOCK, depth - at))
        parts = [in_ref[at : at + have, :]] if have else []
        if have < BLOCK:
            parts.append(jnp.zeros((BLOCK - have, rows), in_ref.dtype))
        part = jnp.concatenate(parts, 0) if len(parts) > 1 else parts[0]
        out_ref[:, at : at + BLOCK] = part.T


def widen(activations):
    rows, depth = activations.shape
    return pl.pallas_call(
        widen_kernel,
        out_shape=jax.ShapeDtypeStruct((rows, depth + -depth % WIDE), activations.dtype),
        in_specs=[VMEM],
        out_specs=VMEM,
        cost_estimate=LITTLE,
    )(activations.T)


def project_kernel(where_ref, *refs):
    count = len(refs) - 5
    pieces, basis_ref, farthest_ref, shares_ref, held, sems = refs[:count], *refs[count:]
    z = where_ref[3]
    row, blocks = 0, {}
    for i, piece in enumerate(pieces):
        load = pltpu.make_async_copy(piece, held.at[row : row + piece.shape[0]], sems.at[i])
        load.start()
        blocks.setdefault(row // BLOCK, []).append(load)
        row += piece.shape[0]
    for block, loads in blocks.items():
        for load in loads:
            load.wait()
        tokens = held[block * BLOCK : (block + 1) * BLOCK]
        place = lax.rem(block - z + 3 + Z, Z)
        shares_ref[pl.ds(pl.multiple_of(place * BLOCK, BLOCK), BLOCK), :] = jnp.dot(
            tokens, basis_ref[...], preferred_element_type=f32
        )
    farthest_ref[...] = shares_ref[(Z - 1) * BLOCK :, :].astype(bf16)


def project(where, pieces, basis):
    rows = sum(piece.shape[0] for piece in pieces)
    depth, wide = basis.shape
    return pl.pallas_call(
        project_kernel,
        out_shape=[jax.ShapeDtypeStruct((BLOCK, wide), bf16), jax.ShapeDtypeStruct((rows, wide), f32)],
        in_specs=[SMEM] + [ANY] * len(pieces) + [VMEM],
        out_specs=[VMEM, VMEM],
        scratch_shapes=[pltpu.VMEM((rows, depth), bf16), pltpu.SemaphoreType.DMA((len(pieces),))],
        compiler_params=pltpu.CompilerParams(vmem_limit_bytes=24 * 1024 * 1024),
        cost_estimate=LITTLE,
    )(where, *pieces, basis)


class Stream:
    def __init__(self, order, farthest, shares):
        self.order = order
        self.farthest = farthest
        self.shares = shares
        self.left = 4
        self.blocks = {}

    def share(self, k):
        place = (k + 3) % Z
        return self.shares[place * BLOCK : (place + 1) * BLOCK]

    def reduce(self):
        k = self.left
        if k == 4:
            low, high = self.farthest[:HALF], self.farthest[HALF:]
        else:
            down, up = self.order(self.down, self.up)
            low, high = self.share(-k), self.share(k)
            if k == 3:
                low = jnp.concatenate([low[:HALF] + down, low[HALF:]], 0)
                high = jnp.concatenate([high[:HALF], high[HALF:] + up], 0)
            else:
                low, high = low + down, high + up
            low, high = low.astype(bf16), high.astype(bf16)
        low, high = self.order(low, high)
        self.down, self.up = shift_z(low, -1), shift_z(high, 1)
        self.left -= 1

    def cross(self):
        down, up = self.order(self.down, self.up)
        self.total = self.share(0) + down + up
        (sent,) = self.order(self.total.astype(bf16))
        self.crossed = swap_x(sent)

    def finish(self):
        (crossed,) = self.order(self.crossed)
        (own,) = self.order((self.total + crossed).astype(bf16))
        self.blocks[0] = own
        self.down, self.up = shift_z(own, -1), shift_z(own, 1)
        self.step = 1

    def spread(self):
        k = self.step
        down, up = self.order(self.down, self.up)
        self.blocks[k], self.blocks[-k] = down, up
        if k == 3:
            down, up = down[:HALF], up[HALF:]
        self.down, self.up = shift_z(down, -1), shift_z(up, 1)
        self.step += 1

    def arrive(self):
        self.blocks[4] = tuple(self.order(self.down, self.up))


def outer_kernel(scale, which, earlier, parts_of, where_ref, lengths_ref, places_ref, grads_ref, *refs):
    acts, out_ref = refs[: sum(parts_of)], refs[-1]
    high, block = grads_ref.shape[1:]
    y, x, c, z = (where_ref[i] for i in range(4))
    token = lax.broadcasted_iota(jnp.int32, (high, block), 1)
    first = 0
    for i, (s, k) in enumerate(which):
        place = lax.rem(z + k + Z, Z) + s * Z
        at = lax.rem(y + places_ref[place, 0] + Y, Y) * X_LO + lax.rem(x + places_ref[place, 1], X_LO)
        at = at * CORE + lax.rem(c + places_ref[place, 2], CORE)
        grads = grads_ref[places_ref[place, 3]]
        zeros = jnp.zeros_like(grads)
        masked, begin = [], jnp.int32(0)
        for e in range(EXB):
            end = begin + lengths_ref[at, e]
            masked.append(jnp.where((token >= begin) & (token < end), grads, zeros))
            begin = end
        lhs = jnp.concatenate(masked, axis=0)
        parts = acts[first : first + parts_of[i]]
        first += parts_of[i]
        for n in range(0, out_ref.shape[1], WIDE):
            columns = slice(n, min(n + WIDE, out_ref.shape[1]))
            rhs = [part[:, columns] for part in parts]
            rhs = jnp.concatenate(rhs, axis=0) if len(rhs) > 1 else rhs[0]
            coeffs = jnp.dot(lhs, rhs, preferred_element_type=f32)
            squares = coeffs * coeffs
            total = squares[:high]
            for e in range(1, EXB):
                total = total + squares[e * high : (e + 1) * high]
            if i:
                total = total + out_ref[:, columns]
            elif earlier:
                total = total + refs[len(acts)][:, columns]
            if scale is not None and i == len(which) - 1:
                total = total * scale
            out_ref[:, columns] = total


def squared_sums(which, where, places, streams, lengths, grads, earlier, scale=None):
    high = grads.shape[1]
    parts = [p if isinstance(p, tuple) else (p,) for p in (streams[s].blocks[k] for s, k in which)]
    parts_of = tuple(len(p) for p in parts)
    acts = [a for p in parts for a in p]
    earlier = [] if earlier is None else [earlier]
    places = jnp.array(places, jnp.int32)
    return pl.pallas_call(
        lambda *refs: outer_kernel(scale, which, bool(earlier), parts_of, *refs),
        out_shape=jax.ShapeDtypeStruct((high, acts[0].shape[1]), f32),
        in_specs=[SMEM] * 3 + [VMEM] * (1 + len(acts) + len(earlier)),
        out_specs=VMEM,
        compiler_params=pltpu.CompilerParams(vmem_limit_bytes=16 * 1024 * 1024),
        cost_estimate=LITTLE,
    )(where, lengths, places, grads, *acts, *earlier)


def on_device(activations, out_grads, act_basis, grad_basis, ex_lengths):
    token_count = out_grads.shape[0] * lax.axis_size("ex")
    z = lax.axis_index("basis") % Z
    ex = lax.axis_index("ex")
    where = jnp.stack([ex // (X_LO * CORE), (ex // CORE) % X_LO, ex % CORE, z]).astype(jnp.int32)
    lengths = ex_lengths.astype(jnp.int32)

    order = Order(where)

    own = widen(activations)
    from_down = shift_ex(own, 1, 0, 0)
    from_up = shift_ex(own, -1, 0, 0)
    beside = shift_ex(own, 0, 1, 0)
    own_other = other_core(own)
    grad_local = lax.dot_general(
        grad_basis, out_grads, (((0,), (1,)), ((), ())), preferred_element_type=f32
    ).astype(bf16)
    basis = jnp.pad(act_basis, ((0, own.shape[1] - act_basis.shape[0]), (0, 0)))
    grad_local, basis = order(grad_local, basis)
    from_down, from_up, beside = order(from_down, from_up, beside)
    far = shift_ex(from_down, 1, 0, 0)
    beside_up = shift_ex(beside, -1, 0, 0)
    beside_down = shift_ex(from_down, 0, 1, 0)
    second = [from_down, from_up, beside]
    second_other = [other_core(p) for p in second]
    a = Stream(order, *order(*project(where, [own, own_other, *second, *second_other], basis)))
    grad_beside = shift_ex(grad_local, 0, 1, 0)
    far, beside_up, beside_down = order(far, beside_up, beside_down)
    last = order(beside_down[:HALF], beside_up[HALF:])
    last = [shift_ex(last[0], 1, 0, 0), shift_ex(last[1], -1, 0, 0)]
    third = [far, beside_up, beside_down]
    third_other = [other_core(p) for p in third]
    a.reduce()
    (grad_beside,) = order(grad_beside)
    grads = jnp.stack([grad_local, grad_beside])
    grads_other = other_core(grads)
    last = order(*last)
    last_other = [other_core(p) for p in last]
    a.reduce()
    b = Stream(order, *order(*project(where, [*third, *third_other, *last, *last_other], basis)))

    streams = a, b
    ring = [(0, 0)], [(-1, 0), (1, 0), (0, 1)], [(2, 0), (1, 1), (-1, 1)], [(2, 1)]
    held = {0: 0, -1: 1, 1: 2, 2: 3}
    places = [
        (dy, dx, dc, (held[dy] * CORE + dc) * X_LO + dx)
        for group in ring
        for dc in range(CORE)
        for dy, dx in group
    ]
    total = None

    def add(which, scale=None):
        (total_then,) = order(
            squared_sums(which, order.token, places, streams, lengths, grads, total, scale)
        )
        return total_then

    b.reduce()
    a.reduce()
    (grads_other,) = order(grads_other)
    grads = jnp.concatenate([grads, grads_other], 0)
    grads_down, grads_up = shift_ex(grads, 1, 0, 0), shift_ex(grads, -1, 0, 0)
    b.reduce()
    a.reduce()
    grads_down, grads_up = order(grads_down, grads_up)
    grads_far = shift_ex(grads_down, 1, 0, 0)
    b.reduce()
    a.cross()
    b.reduce()
    a.finish()
    (grads_far,) = order(grads_far)
    grads = jnp.concatenate([grads, grads_down, grads_up, grads_far], 0)
    b.cross()
    a.spread()
    b.finish()
    total = add(((0, 0), (0, 1), (0, -1), (1, 0)))
    for k in (2, 3):
        a.spread()
        b.spread()
        total = add(((0, k), (0, -k), (1, k - 1), (1, 1 - k)))
    a.arrive()
    b.spread()
    total = add(((0, 4), (1, 3), (1, -3)))
    b.arrive()
    return add(((1, 4),), 1.0 / token_count)


def solution(mesh):
    in_specs = (P("ex", "basis"), P("ex", None), P("basis", "ex"), P(None, "basis"), P())
    out_specs = P("basis", "ex")
    return jax.shard_map(
        on_device, mesh=mesh, in_specs=in_specs, out_specs=out_specs, check_vma=False
    )
```

```python
import jax
import jax.numpy as jnp
from jax import lax
from jax.experimental import pallas as pl
from jax.experimental.pallas import tpu as pltpu
from jax.sharding import PartitionSpec as P

Z, X_HI = 8, 2
Y, X_LO, CORE = 4, 2, 2
BLOCK = 128
HALF = BLOCK // 2
EXB = 5
WIDE = 256
bf16, f32 = jnp.bfloat16, jnp.float32
LITTLE = pl.CostEstimate(flops=1, bytes_accessed=1, transcendentals=0)
VMEM = pl.BlockSpec(memory_space=pltpu.VMEM)
SMEM = pl.BlockSpec(memory_space=pltpu.SMEM)
ANY = pl.BlockSpec(memory_space=pl.ANY)


class Order:
    def __init__(self, token):
        self.token = token

    def __call__(self, *values):
        *values, self.token = lax.optimization_barrier((*values, self.token))
        return values


def shift_z(value, by):
    pairs = [(x * Z + z, x * Z + (z + by) % Z) for x in range(X_HI) for z in range(Z)]
    return lax.ppermute(value, "basis", pairs)


def swap_x(value):
    pairs = [(x * Z + z, (1 - x) * Z + z) for x in range(X_HI) for z in range(Z)]
    return lax.ppermute(value, "basis", pairs)


def ex_index(y, x, c):
    return (y * X_LO + x) * CORE + c


def shift_ex(value, dy, dx, dc):
    pairs = [
        (ex_index(y, x, c), ex_index((y + dy) % Y, (x + dx) % X_LO, (c + dc) % CORE))
        for y in range(Y)
        for x in range(X_LO)
        for c in range(CORE)
    ]
    return lax.ppermute(value, "ex", pairs)


def other_core(value):
    return shift_ex(value, 0, 0, 1)


def widen_kernel(in_ref, out_ref):
    depth, rows = in_ref.shape
    for at in range(0, out_ref.shape[1], BLOCK):
        have = max(0, min(BLOCK, depth - at))
        parts = [in_ref[at : at + have, :]] if have else []
        if have < BLOCK:
            parts.append(jnp.zeros((BLOCK - have, rows), in_ref.dtype))
        part = jnp.concatenate(parts, 0) if len(parts) > 1 else parts[0]
        out_ref[:, at : at + BLOCK] = part.T


def widen(activations):
    rows, depth = activations.shape
    return pl.pallas_call(
        widen_kernel,
        out_shape=jax.ShapeDtypeStruct((rows, depth + -depth % WIDE), activations.dtype),
        in_specs=[VMEM],
        out_specs=VMEM,
        cost_estimate=LITTLE,
    )(activations.T)


def project_kernel(where_ref, *refs):
    *pieces, basis_ref, farthest_ref, shares_ref = refs
    z = where_ref[3]
    row, blocks = 0, {}
    for piece in pieces:
        blocks.setdefault(row // BLOCK, []).append(piece)
        row += piece.shape[0]
    for block, parts in blocks.items():
        parts = [part[...] for part in parts]
        tokens = jnp.concatenate(parts, 0) if len(parts) > 1 else parts[0]
        place = lax.rem(block - z + 3 + Z, Z)
        shares_ref[pl.ds(pl.multiple_of(place * BLOCK, BLOCK), BLOCK), :] = jnp.dot(
            tokens, basis_ref[...], preferred_element_type=f32
        )
    farthest_ref[...] = shares_ref[(Z - 1) * BLOCK :, :].astype(bf16)


def project(where, pieces, basis):
    rows = sum(piece.shape[0] for piece in pieces)
    wide = basis.shape[1]
    return pl.pallas_call(
        project_kernel,
        out_shape=[jax.ShapeDtypeStruct((BLOCK, wide), bf16), jax.ShapeDtypeStruct((rows, wide), f32)],
        in_specs=[SMEM] + [VMEM] * (len(pieces) + 1),
        out_specs=[VMEM, VMEM],
        compiler_params=pltpu.CompilerParams(vmem_limit_bytes=20 * 1024 * 1024),
        cost_estimate=LITTLE,
    )(where, *pieces, basis)


class Stream:
    def __init__(self, order, farthest, shares):
        self.order = order
        self.farthest = farthest
        self.shares = shares
        self.left = 4
        self.blocks = {}

    def share(self, k):
        place = (k + 3) % Z
        return self.shares[place * BLOCK : (place + 1) * BLOCK]

    def reduce(self):
        k = self.left
        if k == 4:
            low, high = self.farthest[:HALF], self.farthest[HALF:]
        else:
            down, up = self.order(self.down, self.up)
            low, high = self.share(-k), self.share(k)
            if k == 3:
                low = jnp.concatenate([low[:HALF] + down, low[HALF:]], 0)
                high = jnp.concatenate([high[:HALF], high[HALF:] + up], 0)
            else:
                low, high = low + down, high + up
            low, high = low.astype(bf16), high.astype(bf16)
        low, high = self.order(low, high)
        self.down, self.up = shift_z(low, -1), shift_z(high, 1)
        self.left -= 1

    def cross(self):
        down, up = self.order(self.down, self.up)
        self.total = self.share(0) + down + up
        (sent,) = self.order(self.total.astype(bf16))
        self.crossed = swap_x(sent)

    def finish(self):
        (crossed,) = self.order(self.crossed)
        (own,) = self.order((self.total + crossed).astype(bf16))
        self.blocks[0] = own
        self.down, self.up = shift_z(own, -1), shift_z(own, 1)
        self.step = 1

    def spread(self):
        k = self.step
        down, up = self.order(self.down, self.up)
        self.blocks[k], self.blocks[-k] = down, up
        if k == 3:
            down, up = down[:HALF], up[HALF:]
        self.down, self.up = shift_z(down, -1), shift_z(up, 1)
        self.step += 1

    def arrive(self):
        self.blocks[4] = tuple(self.order(self.down, self.up))


def outer_kernel(scale, which, earlier, parts_of, where_ref, lengths_ref, places_ref, grads_ref, *refs):
    acts, out_ref = refs[: sum(parts_of)], refs[-1]
    high, block = grads_ref.shape[1:]
    y, x, c, z = (where_ref[i] for i in range(4))
    token = lax.broadcasted_iota(jnp.int32, (high, block), 1)
    first = 0
    for i, (s, k) in enumerate(which):
        place = lax.rem(z + k + Z, Z) + s * Z
        at = lax.rem(y + places_ref[place, 0] + Y, Y) * X_LO + lax.rem(x + places_ref[place, 1], X_LO)
        at = at * CORE + lax.rem(c + places_ref[place, 2], CORE)
        grads = grads_ref[places_ref[place, 3]]
        zeros = jnp.zeros_like(grads)
        masked, begin = [], jnp.int32(0)
        for e in range(EXB):
            end = begin + lengths_ref[at, e]
            masked.append(jnp.where((token >= begin) & (token < end), grads, zeros))
            begin = end
        lhs = jnp.concatenate(masked, axis=0)
        parts = acts[first : first + parts_of[i]]
        first += parts_of[i]
        for n in range(0, out_ref.shape[1], WIDE):
            columns = slice(n, min(n + WIDE, out_ref.shape[1]))
            rhs = [part[:, columns] for part in parts]
            rhs = jnp.concatenate(rhs, axis=0) if len(rhs) > 1 else rhs[0]
            coeffs = jnp.dot(lhs, rhs, preferred_element_type=f32)
            squares = coeffs * coeffs
            total = squares[:high]
            for e in range(1, EXB):
                total = total + squares[e * high : (e + 1) * high]
            if i:
                total = total + out_ref[:, columns]
            elif earlier:
                total = total + refs[len(acts)][:, columns]
            if scale is not None and i == len(which) - 1:
                total = total * scale
            out_ref[:, columns] = total


def squared_sums(which, where, places, streams, lengths, grads, earlier, scale=None):
    high = grads.shape[1]
    parts = [p if isinstance(p, tuple) else (p,) for p in (streams[s].blocks[k] for s, k in which)]
    parts_of = tuple(len(p) for p in parts)
    acts = [a for p in parts for a in p]
    earlier = [] if earlier is None else [earlier]
    places = jnp.array(places, jnp.int32)
    return pl.pallas_call(
        lambda *refs: outer_kernel(scale, which, bool(earlier), parts_of, *refs),
        out_shape=jax.ShapeDtypeStruct((high, acts[0].shape[1]), f32),
        in_specs=[SMEM] * 3 + [VMEM] * (1 + len(acts) + len(earlier)),
        out_specs=VMEM,
        compiler_params=pltpu.CompilerParams(vmem_limit_bytes=16 * 1024 * 1024),
        cost_estimate=LITTLE,
    )(where, lengths, places, grads, *acts, *earlier)


def on_device(activations, out_grads, act_basis, grad_basis, ex_lengths):
    token_count = out_grads.shape[0] * lax.axis_size("ex")
    z = lax.axis_index("basis") % Z
    ex = lax.axis_index("ex")
    where = jnp.stack([ex // (X_LO * CORE), (ex // CORE) % X_LO, ex % CORE, z]).astype(jnp.int32)
    lengths = ex_lengths.astype(jnp.int32)

    order = Order(where)

    own = widen(activations)
    from_down = shift_ex(own, 1, 0, 0)
    from_up = shift_ex(own, -1, 0, 0)
    beside = shift_ex(own, 0, 1, 0)
    own_other = other_core(own)
    grad_local = lax.dot_general(
        grad_basis, out_grads, (((0,), (1,)), ((), ())), preferred_element_type=f32
    ).astype(bf16)
    basis = jnp.pad(act_basis, ((0, own.shape[1] - act_basis.shape[0]), (0, 0)))
    grad_local, basis = order(grad_local, basis)
    from_down, from_up, beside = order(from_down, from_up, beside)
    far = shift_ex(from_down, 1, 0, 0)
    beside_up = shift_ex(beside, -1, 0, 0)
    beside_down = shift_ex(from_down, 0, 1, 0)
    second = [from_down, from_up, beside]
    second_other = [other_core(p) for p in second]
    a = Stream(order, *order(*project(where, [own, own_other, *second, *second_other], basis)))
    grad_beside = shift_ex(grad_local, 0, 1, 0)
    far, beside_up, beside_down = order(far, beside_up, beside_down)
    last = order(beside_down[:HALF], beside_up[HALF:])
    last = [shift_ex(last[0], 1, 0, 0), shift_ex(last[1], -1, 0, 0)]
    third = [far, beside_up, beside_down]
    third_other = [other_core(p) for p in third]
    a.reduce()
    (grad_beside,) = order(grad_beside)
    grads = jnp.stack([grad_local, grad_beside])
    grads_other = other_core(grads)
    last = order(*last)
    last_other = [other_core(p) for p in last]
    a.reduce()
    b = Stream(order, *order(*project(where, [*third, *third_other, *last, *last_other], basis)))

    streams = a, b
    ring = [(0, 0)], [(-1, 0), (1, 0), (0, 1)], [(2, 0), (1, 1), (-1, 1)], [(2, 1)]
    held = {0: 0, -1: 1, 1: 2, 2: 3}
    places = [
        (dy, dx, dc, (held[dy] * CORE + dc) * X_LO + dx)
        for group in ring
        for dc in range(CORE)
        for dy, dx in group
    ]
    total = None

    def add(which, scale=None):
        (total_then,) = order(
            squared_sums(which, order.token, places, streams, lengths, grads, total, scale)
        )
        return total_then

    b.reduce()
    a.reduce()
    (grads_other,) = order(grads_other)
    grads = jnp.concatenate([grads, grads_other], 0)
    grads_down, grads_up = shift_ex(grads, 1, 0, 0), shift_ex(grads, -1, 0, 0)
    b.reduce()
    a.reduce()
    grads_down, grads_up = order(grads_down, grads_up)
    grads_far = shift_ex(grads_down, 1, 0, 0)
    b.reduce()
    a.cross()
    b.reduce()
    a.finish()
    (grads_far,) = order(grads_far)
    grads = jnp.concatenate([grads, grads_down, grads_up, grads_far], 0)
    b.cross()
    a.spread()
    b.finish()
    total = add(((0, 0), (0, 1), (0, -1), (1, 0)))
    for k in (2, 3):
        a.spread()
        b.spread()
        total = add(((0, k), (0, -k), (1, k - 1), (1, 1 - k)))
    a.arrive()
    b.spread()
    total = add(((0, 4), (1, 3), (1, -3)))
    b.arrive()
    return add(((1, 4),), 1.0 / token_count)


def solution(mesh):
    in_specs = (P("ex", "basis"), P("ex", None), P("basis", "ex"), P(None, "basis"), P())
    out_specs = P("basis", "ex")
    return jax.shard_map(
        on_device, mesh=mesh, in_specs=in_specs, out_specs=out_specs, check_vma=False
    )
```

```python
import jax
import jax.numpy as jnp
from jax import lax
from jax.experimental import pallas as pl
from jax.experimental.pallas import tpu as pltpu
from jax.sharding import PartitionSpec as P

Z, X_HI = 8, 2
Y, X_LO, CORE = 4, 2, 2
BLOCK = 128
HALF = BLOCK // 2
EXB = 5
WIDE = 256
bf16, f32 = jnp.bfloat16, jnp.float32
LITTLE = pl.CostEstimate(flops=1, bytes_accessed=1, transcendentals=0)
VMEM = pl.BlockSpec(memory_space=pltpu.VMEM)
SMEM = pl.BlockSpec(memory_space=pltpu.SMEM)
ANY = pl.BlockSpec(memory_space=pl.ANY)


class Order:
    def __init__(self, token):
        self.token = token

    def __call__(self, *values):
        *values, self.token = lax.optimization_barrier((*values, self.token))
        return values


def shift_z(value, by):
    pairs = [(x * Z + z, x * Z + (z + by) % Z) for x in range(X_HI) for z in range(Z)]
    return lax.ppermute(value, "basis", pairs)


def swap_x(value):
    pairs = [(x * Z + z, (1 - x) * Z + z) for x in range(X_HI) for z in range(Z)]
    return lax.ppermute(value, "basis", pairs)


def ex_index(y, x, c):
    return (y * X_LO + x) * CORE + c


def shift_ex(value, dy, dx, dc):
    pairs = [
        (ex_index(y, x, c), ex_index((y + dy) % Y, (x + dx) % X_LO, (c + dc) % CORE))
        for y in range(Y)
        for x in range(X_LO)
        for c in range(CORE)
    ]
    return lax.ppermute(value, "ex", pairs)


def other_core(value):
    return shift_ex(value, 0, 0, 1)


def widen_kernel(in_ref, out_ref):
    depth, rows = in_ref.shape
    for at in range(0, out_ref.shape[1], BLOCK):
        have = max(0, min(BLOCK, depth - at))
        parts = [in_ref[at : at + have, :]] if have else []
        if have < BLOCK:
            parts.append(jnp.zeros((BLOCK - have, rows), in_ref.dtype))
        part = jnp.concatenate(parts, 0) if len(parts) > 1 else parts[0]
        out_ref[:, at : at + BLOCK] = part.T


def widen(activations):
    rows, depth = activations.shape
    return pl.pallas_call(
        widen_kernel,
        out_shape=jax.ShapeDtypeStruct((rows, depth + -depth % WIDE), activations.dtype),
        in_specs=[VMEM],
        out_specs=VMEM,
        cost_estimate=LITTLE,
    )(activations.T)


def project_kernel(where_ref, *refs):
    *pieces, basis_ref, farthest_ref, shares_ref = refs
    z = where_ref[3]
    row, blocks = 0, {}
    for piece in pieces:
        blocks.setdefault(row // BLOCK, []).append(piece)
        row += piece.shape[0]
    for block, parts in blocks.items():
        parts = [part[...] for part in parts]
        tokens = jnp.concatenate(parts, 0) if len(parts) > 1 else parts[0]
        place = lax.rem(block - z + 3 + Z, Z)
        shares_ref[pl.ds(pl.multiple_of(place * BLOCK, BLOCK), BLOCK), :] = jnp.dot(
            tokens, basis_ref[...], preferred_element_type=f32
        )
    farthest_ref[...] = shares_ref[(Z - 1) * BLOCK :, :].astype(bf16)


def project(where, pieces, basis):
    rows = sum(piece.shape[0] for piece in pieces)
    wide = basis.shape[1]
    return pl.pallas_call(
        project_kernel,
        out_shape=[jax.ShapeDtypeStruct((BLOCK, wide), bf16), jax.ShapeDtypeStruct((rows, wide), f32)],
        in_specs=[SMEM] + [VMEM] * (len(pieces) + 1),
        out_specs=[VMEM, VMEM],
        compiler_params=pltpu.CompilerParams(vmem_limit_bytes=20 * 1024 * 1024),
        cost_estimate=LITTLE,
    )(where, *pieces, basis)


class Stream:
    def __init__(self, order, farthest, shares):
        self.order = order
        self.farthest = farthest
        self.shares = shares
        self.left = 4
        self.blocks = {}

    def share(self, k):
        place = (k + 3) % Z
        return self.shares[place * BLOCK : (place + 1) * BLOCK]

    def reduce(self):
        k = self.left
        if k == 4:
            low, high = self.farthest[:HALF], self.farthest[HALF:]
        else:
            down, up = self.order(self.down, self.up)
            low, high = self.share(-k), self.share(k)
            if k == 3:
                low = jnp.concatenate([low[:HALF] + down, low[HALF:]], 0)
                high = jnp.concatenate([high[:HALF], high[HALF:] + up], 0)
            else:
                low, high = low + down, high + up
            low, high = low.astype(bf16), high.astype(bf16)
        low, high = self.order(low, high)
        self.down, self.up = shift_z(low, -1), shift_z(high, 1)
        self.left -= 1

    def cross(self):
        down, up = self.order(self.down, self.up)
        self.total = self.share(0) + down + up
        (sent,) = self.order(self.total.astype(bf16))
        self.crossed = swap_x(sent)

    def finish(self):
        (crossed,) = self.order(self.crossed)
        (own,) = self.order((self.total + crossed).astype(bf16))
        self.blocks[0] = own
        self.down, self.up = shift_z(own, -1), shift_z(own, 1)
        self.step = 1

    def spread(self):
        k = self.step
        down, up = self.order(self.down, self.up)
        self.blocks[k], self.blocks[-k] = down, up
        if k == 3:
            down, up = down[:HALF], up[HALF:]
        self.down, self.up = shift_z(down, -1), shift_z(up, 1)
        self.step += 1

    def arrive(self):
        self.blocks[4] = tuple(self.order(self.down, self.up))


def outer_kernel(scale, which, earlier, parts_of, where_ref, lengths_ref, places_ref, grads_ref, *refs):
    acts, out_ref = refs[: sum(parts_of)], refs[-1]
    high, block = grads_ref.shape[1:]
    y, x, c, z = (where_ref[i] for i in range(4))
    token = lax.broadcasted_iota(jnp.int32, (high, block), 1)
    first = 0
    for i, (s, k) in enumerate(which):
        place = lax.rem(z + k + Z, Z) + s * Z
        at = lax.rem(y + places_ref[place, 0] + Y, Y) * X_LO + lax.rem(x + places_ref[place, 1], X_LO)
        at = at * CORE + lax.rem(c + places_ref[place, 2], CORE)
        grads = grads_ref[places_ref[place, 3]]
        zeros = jnp.zeros_like(grads)
        masked, begin = [], jnp.int32(0)
        for e in range(EXB):
            end = begin + lengths_ref[at, e]
            masked.append(jnp.where((token >= begin) & (token < end), grads, zeros))
            begin = end
        lhs = jnp.concatenate(masked, axis=0)
        parts = acts[first : first + parts_of[i]]
        first += parts_of[i]
        for n in range(0, out_ref.shape[1], WIDE):
            columns = slice(n, min(n + WIDE, out_ref.shape[1]))
            rhs = [part[:, columns] for part in parts]
            rhs = jnp.concatenate(rhs, axis=0) if len(rhs) > 1 else rhs[0]
            coeffs = jnp.dot(lhs, rhs, preferred_element_type=f32)
            squares = coeffs * coeffs
            total = squares[:high]
            for e in range(1, EXB):
                total = total + squares[e * high : (e + 1) * high]
            if i:
                total = total + out_ref[:, columns]
            elif earlier:
                total = total + refs[len(acts)][:, columns]
            if scale is not None and i == len(which) - 1:
                total = total * scale
            out_ref[:, columns] = total


def squared_sums(which, where, places, streams, lengths, grads, earlier, scale=None):
    high = grads.shape[1]
    parts = [p if isinstance(p, tuple) else (p,) for p in (streams[s].blocks[k] for s, k in which)]
    parts_of = tuple(len(p) for p in parts)
    acts = [a for p in parts for a in p]
    earlier = [] if earlier is None else [earlier]
    places = jnp.array(places, jnp.int32)
    return pl.pallas_call(
        lambda *refs: outer_kernel(scale, which, bool(earlier), parts_of, *refs),
        out_shape=jax.ShapeDtypeStruct((high, acts[0].shape[1]), f32),
        in_specs=[SMEM] * 3 + [VMEM] * (1 + len(acts) + len(earlier)),
        out_specs=VMEM,
        compiler_params=pltpu.CompilerParams(vmem_limit_bytes=16 * 1024 * 1024),
        cost_estimate=LITTLE,
    )(where, lengths, places, grads, *acts, *earlier)


def on_device(activations, out_grads, act_basis, grad_basis, ex_lengths):
    token_count = out_grads.shape[0] * lax.axis_size("ex")
    z = lax.axis_index("basis") % Z
    ex = lax.axis_index("ex")
    where = jnp.stack([ex // (X_LO * CORE), (ex // CORE) % X_LO, ex % CORE, z]).astype(jnp.int32)
    lengths = ex_lengths.astype(jnp.int32)

    order = Order(where)

    own = widen(activations)
    from_down = shift_ex(own, 1, 0, 0)
    from_up = shift_ex(own, -1, 0, 0)
    beside = shift_ex(own, 0, 1, 0)
    own_other = other_core(own)
    grad_local = lax.dot_general(
        grad_basis, out_grads, (((0,), (1,)), ((), ())), preferred_element_type=f32
    ).astype(bf16)
    basis = jnp.pad(act_basis, ((0, own.shape[1] - act_basis.shape[0]), (0, 0)))
    grad_local, basis = order(grad_local, basis)
    from_down, from_up, beside = order(from_down, from_up, beside)
    far = shift_ex(from_down, 1, 0, 0)
    beside_up = shift_ex(beside, -1, 0, 0)
    beside_down = shift_ex(from_down, 0, 1, 0)
    second = [from_down, from_up, beside]
    second_other = [other_core(p) for p in second]
    a = Stream(order, *order(*project(where, [own, own_other, *second, *second_other], basis)))
    grad_beside = shift_ex(grad_local, 0, 1, 0)
    far, beside_up, beside_down = order(far, beside_up, beside_down)
    last = order(beside_down[:HALF], beside_up[HALF:])
    last = [shift_ex(last[0], 1, 0, 0), shift_ex(last[1], -1, 0, 0)]
    third = [far, beside_up, beside_down]
    third_other = [other_core(p) for p in third]
    a.reduce()
    (grad_beside,) = order(grad_beside)
    grads = jnp.stack([grad_local, grad_beside])
    grads_other = other_core(grads)
    last = order(*last)
    last_other = [other_core(p) for p in last]
    a.reduce()
    b = Stream(order, *order(*project(where, [*third, *third_other, *last, *last_other], basis)))

    streams = a, b
    ring = [(0, 0)], [(-1, 0), (1, 0), (0, 1)], [(2, 0), (1, 1), (-1, 1)], [(2, 1)]
    held = {0: 0, -1: 1, 1: 2, 2: 3}
    places = [
        (dy, dx, dc, (held[dy] * CORE + dc) * X_LO + dx)
        for group in ring
        for dc in range(CORE)
        for dy, dx in group
    ]
    total = None

    def add(which, scale=None):
        (total_then,) = order(
            squared_sums(which, order.token, places, streams, lengths, grads, total, scale)
        )
        return total_then

    b.reduce()
    a.reduce()
    b.reduce()
    (grads_other,) = order(grads_other)
    grads = jnp.concatenate([grads, grads_other], 0)
    grads_down, grads_up = shift_ex(grads, 1, 0, 0), shift_ex(grads, -1, 0, 0)
    a.reduce()
    b.reduce()
    grads_down, grads_up = order(grads_down, grads_up)
    grads_far = shift_ex(grads_down, 1, 0, 0)
    a.cross()
    b.reduce()
    a.finish()
    (grads_far,) = order(grads_far)
    grads = jnp.concatenate([grads, grads_down, grads_up, grads_far], 0)
    b.cross()
    a.spread()
    b.finish()
    total = add(((0, 0), (0, 1), (0, -1), (1, 0)))
    for k in (2, 3):
        a.spread()
        b.spread()
        total = add(((0, k), (0, -k), (1, k - 1), (1, 1 - k)))
    a.arrive()
    b.spread()
    total = add(((0, 4), (1, 3), (1, -3)))
    b.arrive()
    return add(((1, 4),), 1.0 / token_count)


def solution(mesh):
    in_specs = (P("ex", "basis"), P("ex", None), P("basis", "ex"), P(None, "basis"), P())
    out_specs = P("basis", "ex")
    return jax.shard_map(
        on_device, mesh=mesh, in_specs=in_specs, out_specs=out_specs, check_vma=False
    )
```
